512 devices in a mesh: dp: 32 (over z, x_lo, core), expert: 16 (over y, x_hi).
Axes of the slice: x: 4 (x_hi: 2, x_lo: 2; x = x_hi * 2 + x_lo), y: 8, z: 8, core: 2. Of those that a mesh axis runs over, the one named last changes fastest.
Arguments:
- grad_parts: bfloat16 [16, 32, 5120, 128], P('expert', 'dp'), may hold values from -3 to 3
- master: float32 [16, 5120, 128], P('expert', 'dp'), may hold values from -0.3125 to 0.3125
- moment: float32 [16, 5120, 128], P('expert', 'dp'), may hold values from -3 to 3
- second: float32 [16, 5120, 128], P('expert', 'dp'), may hold values from 0.0001 to 0.01
- down_weight: bfloat16 [16, 5120, 64], P('expert', 'dp'), may hold values from -0.75 to 0.75
- tokens: bfloat16 [65536, 5120], P(('dp', 'expert')), may hold values from -6 to 6
- routes: int32 [65536, 1], P(('dp', 'expert')), may hold values from 0 to 15; in each aligned block of 128 rows (0 to 127, 128 to 255, ...) at most 16 rows name the same one
- probs: float32 [65536], P(('dp', 'expert')), may hold values from 0.3 to 1
Outputs:
- new_master: float32 [16, 5120, 128], P('expert', 'dp')
- new_moment: float32 [16, 5120, 128], P('expert', 'dp')
- mixed: bfloat16 [65536, 5120], P(('dp', 'expert'))
The draws below stay inside these ranges and needn't reach their ends.
Inputs may be any that keep to these rules, and one draw needn't show every extreme that they name: `routes`: among the 128 tokens of one device no expert is named more than 16 times; some expert is named exactly 16 times.
All inputs are finite; a program needn't handle non-finite values.
Results may differ from the reference program's by a relative error of at most 0.029.
Values may be sent and summed in bfloat16 or wider, within the bound.
No kernel may reach another device: no remote copies, remote signals or barrier semaphores. Data moves between devices by JAX's collectives and lax.ppermute only.
A program may use at most 64 MiB of HBM per device.

```python
import math
import jax
import jax.numpy as jnp
import numpy as np
from jax import lax

D = 5120
FW = 64
TOK_DEV = 128
EXPERTS = 16
CAP = 16
TOKENS = 65536
N_DP = 32


def strengthened(entries, own_key, source, target, blocks, factor):
    def block_of(axis_at):
        return (jnp.arange(entries.shape[axis_at]) // (entries.shape[axis_at] // blocks)).reshape((-1,) + (1,) * (entries.ndim - 1 - axis_at))

    one_side = jax.random.permutation(own_key, blocks)[block_of(target)]
    other_side = (block_of(target) + blocks // 2) % blocks
    return jnp.where((block_of(source) == one_side) | (block_of(source) == other_side), factor * entries, entries)


def block_levels(rng, extent, cuts, least, largest):
    def one(dim, shards_of):
        heights = jax.random.uniform(jax.random.fold_in(jax.random.fold_in(rng, 6), dim), (shards_of,), jnp.float32, least / len(cuts), largest / len(cuts))
        return jnp.repeat(jnp.exp(heights), extent[dim] // shards_of).reshape((-1,) + (1,) * (len(extent) - dim - 1))

    loudness = one(*cuts[0])
    for cut in cuts[1:]:
        loudness = loudness * one(*cut)
    return loudness


def shared_out(rng, own, number, rows, count, top, bound, lean):
    ranking = jax.random.permutation(rng, count)
    heavy_load, common = portions_of(count, rows * top, bound, lean, True), portions_of(count, rows * top, bound, lean, False)
    places = jnp.arange(count)

    def named(sizes, offset_by):
        used = int((sizes > 0).sum())
        fixed = max(1, used // 4)
        shifted = fixed + (places - fixed + offset_by * (used - fixed)) % max(1, count - fixed)
        return jnp.zeros((count,), jnp.int32).at[ranking[jnp.where(places < fixed, places, shifted)]].set(jnp.asarray(sizes, jnp.int32))

    sizes = jnp.where(number % 4 == 0, named(heavy_load, number // 4), named(common, number - number // 4 - 1))
    mixed = jax.random.permutation(jax.random.fold_in(own, 3), count)
    donor, sink = mixed[0:count // 2 * 2:2], mixed[1:count // 2 * 2:2]
    margin = jnp.minimum(sizes[donor] - 1, bound - sizes[sink]) // 2
    margin = jnp.where((donor == ranking[0]) | (sink == ranking[0]) | (sizes[sink] == 0), 0, jnp.maximum(margin, 0))
    shifted = jax.random.randint(jax.random.fold_in(own, 4), (count // 2,), 0, 1 << 20) % (margin + 1)
    sizes = sizes.at[donor].add(-shifted).at[sink].add(shifted)
    items = jnp.searchsorted(jnp.cumsum(sizes), jnp.arange(rows * top), side="right").astype(jnp.int32)
    grid = items.reshape(top, rows).T
    grid = grid[jax.random.permutation(jax.random.fold_in(own, 1), rows)]
    offset_by = jax.random.randint(jax.random.fold_in(own, 2), (rows, 1), 0, top)
    return jnp.take_along_axis(grid, (jnp.arange(top)[None, :] + offset_by) % top, axis=1)


def portions_of(amount, total, most, lean, full):
    loads = [(1 << 20) // math.isqrt(standing ** lean) + 1 for standing in range(1, amount + 1)]
    largest = most if full else min(most, max(-(-total // amount), total * loads[0] // sum(loads)))
    least = 1 if total - largest >= amount - 1 else 0
    given, surplus = [largest] + [least] * (amount - 1), total - largest - least * (amount - 1)
    while surplus > 0:
        candidates = [i for i in range(1, amount) if given[i] < largest] or [i for i in range(1, amount) if given[i] < most]
        whole, remaining = sum([loads[i] for i in candidates]), surplus
        for i in candidates:
            extra = min(most - given[i], max(1, remaining * loads[i] // whole), surplus)
            given[i] = given[i] + extra
            surplus = surplus - extra
    return np.array(given)


def gaussian(key, shape, deviation, limit, shards=(), kind=jnp.bfloat16):
    array = deviation * jax.random.normal(key, shape, jnp.float32)
    if shards:
        array = array * block_levels(key, shape, shards, -0.22, 0.18)
    return jnp.clip(array, -limit, limit).astype(kind)


def bell_draw_with(key, dims, scale, reach, split, heavy, kind=jnp.bfloat16):
    values = scale * jax.random.normal(key, dims, jnp.float32)
    if split:
        values = values * block_levels(key, dims, split, -0.22, 0.18)
    return jnp.clip(strengthened(values, jax.random.fold_in(key, 3), *heavy), -reach, reach).astype(kind)


def setup_inputs(seed: int = 0) -> dict:
    keys = jax.random.split(jax.random.key(seed), 9)
    grad_parts = bell_draw_with(keys[0], (EXPERTS, N_DP, D, 2 * FW), 0.1, 3.0, ((0, 16), (1, 32)), (1, 2, 32, 2.75))
    master = gaussian(keys[1], (EXPERTS, D, 2 * FW), (6 * FW) ** -0.5, 0.3125, ((0, 16), (1, 32)), jnp.float32)
    moment = gaussian(keys[2], (EXPERTS, D, 2 * FW), 0.2, 3.0, ((0, 16), (1, 32)), jnp.float32)
    second = jnp.clip(jnp.exp(math.log(0.01) - 4.6051702 * jax.random.uniform(keys[3], (EXPERTS, D, 2 * FW), jnp.float32) ** block_levels(keys[3], (EXPERTS, D, 2 * FW), ((0, 16), (1, 32)), -0.2, 0.2)), 0.0001, 0.01)
    down_weight = gaussian(keys[4], (EXPERTS, D, FW), FW ** -0.5, 0.75, ((0, 16), (1, 32)))
    tokens = gaussian(keys[5], (TOKENS, D), 1.0, 6.0, ((0, 512),))
    routes_keys = jax.random.split(jax.random.fold_in(keys[6], 1), TOKENS // TOK_DEV)
    routes_turns = jax.random.permutation(jax.random.fold_in(keys[6], 3), TOKENS // TOK_DEV)
    routes = jax.vmap(lambda own, number: shared_out(jax.random.fold_in(keys[6], 2), own, number, TOK_DEV, EXPERTS, 1, CAP, 2))(routes_keys, routes_turns).reshape((TOKENS, 1))
    probs = jnp.clip(0.3 + 0.7 * jax.random.uniform(keys[7], (TOKENS,), jnp.float32) ** block_levels(keys[7], (TOKENS,), ((0, 512),), -0.2, 0.2), 0.3, 1.0)
    return {"grad_parts": grad_parts, "master": master, "moment": moment, "second": second, "down_weight": down_weight, "tokens": tokens, "routes": routes, "probs": probs}


beta_one = 0.9
beta_two = 0.95
learn_rate = 0.005
decay_rate = 0.1
adam_eps = 1e-08
bias_one = 1.0 - 0.9 ** 50
bias_two = 1.0 - 0.95 ** 50
block_rows = 512

def adamw(weight, moment, second, grad):
    moment_new = beta_one * moment + (1.0 - beta_one) * grad
    second_new = beta_two * second + (1.0 - beta_two) * grad * grad
    update = moment_new / bias_one / (jnp.sqrt(second_new / bias_two) + adam_eps)
    return (weight - learn_rate * (update + decay_rate * weight), moment_new)

def reference(grad_parts, master, moment, second, down_weight, tokens, routes, probs):

    def update_one(items):
        parts, weight, first, last = items
        total = lax.optimization_barrier(jnp.sum(parts.astype(jnp.float32), axis=0))
        return adamw(weight, first, last, total)
    new_master, new_moment = lax.map(update_one, (grad_parts, master, moment, second))
    weights = new_master.astype(jnp.bfloat16)
    chosen = routes[:, 0].astype(jnp.int32)
    order = jnp.argsort(chosen, stable=True).astype(jnp.int32)
    padded = jnp.concatenate([order, jnp.full((block_rows,), TOKENS, jnp.int32)]).astype(jnp.int32)
    counts = lax.optimization_barrier(jnp.sum((chosen[:, None] == jnp.arange(EXPERTS, dtype=jnp.int32)[None, :]).astype(jnp.int32), axis=0))
    starts = (jnp.cumsum(counts) - counts).astype(jnp.int32)

    def expert_rows(index, output):
        gate_up = weights[index]
        down = down_weight[index]
        count = counts[index]
        start = starts[index]

        def one_block(blk, out):
            offset = (start + blk * block_rows).astype(jnp.int32)
            picks = lax.dynamic_slice(padded, (offset,), (block_rows,))
            valid = blk * block_rows + jnp.arange(block_rows, dtype=jnp.int32) < count
            picks = jnp.where(valid, picks, TOKENS).astype(jnp.int32)
            safe = jnp.minimum(picks, TOKENS - 1)
            rows = tokens[safe]
            both = jnp.dot(rows, gate_up, preferred_element_type=jnp.float32)
            hidden = (jax.nn.silu(both[:, :FW]) * both[:, FW:]).astype(jnp.bfloat16)
            result = jnp.dot(hidden, down.T, preferred_element_type=jnp.float32).astype(jnp.bfloat16)
            values = (probs[safe][:, None] * result.astype(jnp.float32)).astype(jnp.bfloat16)
            return out.at[picks].set(values, mode='drop')
        return lax.fori_loop(0, (count + block_rows - 1) // block_rows, one_block, output)
    mixed = lax.fori_loop(0, EXPERTS, expert_rows, jnp.zeros((TOKENS, D), jnp.bfloat16))
    return (new_master, new_moment, mixed)
```

```python
import functools

import jax
import jax.numpy as jnp
from jax import lax
from jax.experimental import pallas as pl
from jax.experimental.pallas import tpu as pltpu
from jax.sharding import Mesh, PartitionSpec as P

beta_one = 0.9
beta_two = 0.95
learn_rate = 0.005
decay_rate = 0.1
adam_eps = 1e-08
bias_one = 1.0 - 0.9**50
bias_two = 1.0 - 0.95**50

Z, XL, C, Y, XH = 8, 2, 2, 8, 2
GROUP = Z * XL
EXPERTS = Y * XH
D = 5120
ROWS = 160
COLS = 320
TOK = 128
UNITS = 64
SWAP = ((0, 1), (1, 0))
LIMIT = 56 * 1024 * 1024

f32 = jnp.float32
bf16 = jnp.bfloat16


def params(**kw):
    return pltpu.CompilerParams(vmem_limit_bytes=LIMIT, **kw)


def cost(flops, nbytes):
    return pl.CostEstimate(flops=flops, bytes_accessed=nbytes, transcendentals=0)


def pack_kernel(x_ref, o_ref):
    x = x_ref[...]
    half = TOK // 2
    for k in range(2):
        part = x[:, k * COLS : (k + 1) * COLS]
        o_ref[k] = jnp.concatenate([part[:half], part[half:]], axis=1)


def pack(tokens):
    return pl.pallas_call(
        pack_kernel,
        out_shape=jax.ShapeDtypeStruct((GROUP, TOK // 2, 2 * COLS), bf16),
        grid=(Z,),
        in_specs=[pl.BlockSpec((TOK, 2 * COLS), lambda i: (0, i))],
        out_specs=pl.BlockSpec((2, TOK // 2, 2 * COLS), lambda i: (i, 0, 0)),
        compiler_params=params(),
        cost_estimate=cost(0, 2 * TOK * D * 2),
    )(tokens)


def add_kernel(c_ref, g_ref, r_ref, route_ref, o_ref):
    total = g_ref[:, 0].astype(f32) + r_ref[...].astype(f32)
    o_ref[:, :ROWS] = total.astype(bf16)
    rows = jnp.broadcast_to(route_ref[...].astype(f32), (16, TOK)).astype(bf16)
    for i in range(o_ref.shape[0]):
        o_ref[i, ROWS:] = rows


def add(core, grads, received, route_row):
    n = 8
    return pl.pallas_call(
        add_kernel,
        out_shape=jax.ShapeDtypeStruct((GROUP, ROWS + 16, TOK), bf16),
        grid_spec=pltpu.PrefetchScalarGridSpec(
            num_scalar_prefetch=1,
            grid=(GROUP // n,),
            in_specs=[
                pl.BlockSpec((n, 1, ROWS, 128), lambda i, c: (i, c[0], 0, 0)),
                pl.BlockSpec((n, ROWS, 128), lambda i, c: (i, 0, 0)),
                pl.BlockSpec((1, TOK), lambda i, c: (0, 0)),
            ],
            out_specs=pl.BlockSpec((n, ROWS + 16, TOK), lambda i, c: (i, 0, 0)),
        ),
        compiler_params=params(),
        cost_estimate=cost(0, 3 * GROUP * ROWS * 256),
    )(core, grads, received, route_row)


def adam_kernel(g_ref, w_ref, m_ref, s_ref, nw_ref, nm_ref, short_ref, route_ref):
    total = g_ref[0, :ROWS].astype(f32)
    for i in range(1, GROUP):
        total = total + g_ref[i, :ROWS].astype(f32)
    weight = w_ref[...]
    moment_new = beta_one * m_ref[...] + (1.0 - beta_one) * total
    second_new = beta_two * s_ref[...] + (1.0 - beta_two) * total * total
    update = moment_new / bias_one / (jnp.sqrt(second_new / bias_two) + adam_eps)
    new_weight = weight - learn_rate * (update + decay_rate * weight)
    nw_ref[...] = new_weight
    nm_ref[...] = moment_new
    short_ref[...] = new_weight.astype(bf16)
    for i in range(GROUP):
        route_ref[i : i + 1, :] = g_ref[i, ROWS : ROWS + 16].astype(f32)[0:1]


def adam(arrived, master, moment, second):
    return pl.pallas_call(
        adam_kernel,
        out_shape=(
            jax.ShapeDtypeStruct((ROWS, 128), f32),
            jax.ShapeDtypeStruct((ROWS, 128), f32),
            jax.ShapeDtypeStruct((ROWS, 128), bf16),
            jax.ShapeDtypeStruct((GROUP, TOK), f32),
        ),
        compiler_params=params(),
        cost_estimate=cost(0, GROUP * ROWS * 256 + 5 * ROWS * 512),
    )(arrived, master, moment, second)


def partial_kernel(ids_ref, own_ref, other_ref, x_ref, route_ref, o_ref, w_scr, x_scr, r_scr, acc_scr):
    core = ids_ref[0]
    high = ids_ref[1]
    half = TOK // 2
    mine = pl.multiple_of(core * ROWS, 32)
    theirs = pl.multiple_of((1 - core) * ROWS, 32)
    for e in range(EXPERTS):
        w_scr[pl.ds(mine, ROWS), e * 128 : (e + 1) * 128] = own_ref[e]
        w_scr[pl.ds(theirs, ROWS), e * 128 : (e + 1) * 128] = other_ref[e]
    columns = jnp.transpose(route_ref[...])
    for s in range(GROUP):
        x_scr[s * TOK : s * TOK + half, :] = x_ref[s, :, :COLS]
        x_scr[s * TOK + half : (s + 1) * TOK, :] = x_ref[s, :, COLS:]
        r_scr[s * TOK : (s + 1) * TOK, :] = jnp.broadcast_to(columns[:, s : s + 1], (TOK, 128))
    step = 512
    for e in range(0, EXPERTS, 2):
        first = (e + high).astype(f32)
        second = (e + 1 - high).astype(f32)

        def rows(i, carry):
            at = pl.ds(pl.multiple_of(i * step, step), step)
            both = jnp.dot(
                x_scr[at, :], w_scr[:, e * 128 : (e + 2) * 128], preferred_element_type=f32
            )
            route = r_scr[at, :]
            kept = acc_scr[at, :] if e else jnp.zeros((step, 128), f32)
            kept = jnp.where(route == first, both[:, :128], kept)
            kept = jnp.where(route == second, both[:, 128:], kept)
            if e + 2 < EXPERTS:
                acc_scr[at, :] = kept
            else:
                o_ref[at, :] = kept.astype(bf16)
            return carry

        lax.fori_loop(0, GROUP * TOK // step, rows, 0)


def partial_sums(ids, own, other, x, route):
    return pl.pallas_call(
        partial_kernel,
        out_shape=jax.ShapeDtypeStruct((GROUP * TOK, 128), bf16),
        in_specs=[pl.BlockSpec(memory_space=pltpu.SMEM)]
        + [pl.BlockSpec(memory_space=pltpu.VMEM)] * 4,
        out_specs=pl.BlockSpec(memory_space=pltpu.VMEM),
        scratch_shapes=[
            pltpu.VMEM((COLS, EXPERTS * 128), bf16),
            pltpu.VMEM((GROUP * TOK, COLS), bf16),
            pltpu.VMEM((GROUP * TOK, 128), f32),
            pltpu.VMEM((GROUP * TOK, 128), f32),
        ],
        compiler_params=params(),
        cost_estimate=cost(2 * GROUP * TOK * COLS * EXPERTS * 128, 4 * 1024 * 1024),
    )(ids, own, other, x, route)


def hidden_kernel(p_ref, route_ref, o_ref):
    total = p_ref[0].astype(f32)
    for i in range(1, GROUP):
        total = total + p_ref[i].astype(f32)
    gate = total[:, :UNITS]
    up = total[:, UNITS:]
    hidden = gate * jax.nn.sigmoid(gate) * up
    route = jnp.broadcast_to(route_ref[...].astype(f32), (TOK, UNITS))
    o_ref[...] = jnp.concatenate([hidden, route], axis=1).astype(bf16)


def hidden_units(parts, route_column):
    return pl.pallas_call(
        hidden_kernel,
        out_shape=jax.ShapeDtypeStruct((TOK, 128), bf16),
        compiler_params=params(),
        cost_estimate=cost(0, GROUP * TOK * 256),
    )(parts, route_column)


def down_kernel(own_ref, other_ref, d_ref, o_own_ref, o_other_ref, h_scr):
    @pl.when(pl.program_id(0) == 0)
    def _():
        lane = lax.broadcasted_iota(jnp.int32, (2 * TOK, 128), 1)
        both = jnp.concatenate([own_ref[...], other_ref[...]], axis=0).astype(f32)
        hidden = jnp.concatenate([both[:, :UNITS], both[:, :UNITS]], axis=1)
        route = jnp.concatenate([both[:, UNITS:], both[:, UNITS:]], axis=1)
        for y in range(Y):
            expert = jnp.where(lane < UNITS, 2.0 * y, 2.0 * y + 1.0)
            h_scr[:, y * 128 : (y + 1) * 128] = jnp.where(route == expert, hidden, 0.0).astype(bf16)

    total = jnp.zeros((2 * TOK, COLS), f32)
    for y in range(0, Y, 2):
        weights = jnp.concatenate([d_ref[0, y], d_ref[0, y + 1]], axis=1)
        total = total + lax.dot_general(
            h_scr[:, y * 128 : (y + 2) * 128],
            weights,
            (((1,), (1,)), ((), ())),
            preferred_element_type=f32,
        )
    o_own_ref[0] = total[:TOK].astype(bf16)
    o_other_ref[0] = total[TOK:].astype(bf16)


def down_project(own, other, down):
    return pl.pallas_call(
        down_kernel,
        out_shape=(
            jax.ShapeDtypeStruct((Z, TOK, COLS), bf16),
            jax.ShapeDtypeStruct((Z, TOK, COLS), bf16),
        ),
        grid=(Z,),
        in_specs=[
            pl.BlockSpec((TOK, 128), lambda i: (0, 0)),
            pl.BlockSpec((TOK, 128), lambda i: (0, 0)),
            pl.BlockSpec((1, Y, COLS, 128), lambda i: (i, 0, 0, 0)),
        ],
        out_specs=(
            pl.BlockSpec((1, TOK, COLS), lambda i: (i, 0, 0)),
            pl.BlockSpec((1, TOK, COLS), lambda i: (i, 0, 0)),
        ),
        scratch_shapes=[pltpu.VMEM((2 * TOK, EXPERTS * UNITS), bf16)],
        compiler_params=params(),
        cost_estimate=cost(2 * 2 * TOK * 1024 * 2560, 8 * 1024 * 1024),
    )(own, other, down)


def mix_kernel(c_ref, own_ref, other_ref, p_ref, o_ref):
    first_core = c_ref[0] == 0
    own = own_ref[0].astype(f32)
    other = other_ref[0].astype(f32)
    even = jnp.where(first_core, own, other)
    odd = jnp.where(first_core, other, own)
    whole = jnp.concatenate(
        [even[:, :ROWS], odd[:, :ROWS], even[:, ROWS:], odd[:, ROWS:]], axis=1
    )
    o_ref[...] = (p_ref[...] * whole).astype(bf16)


def mix(core, own, other, probs):
    return pl.pallas_call(
        mix_kernel,
        out_shape=jax.ShapeDtypeStruct((TOK, D), bf16),
        grid=(Z,),
        in_specs=[
            pl.BlockSpec(memory_space=pltpu.SMEM),
            pl.BlockSpec((1, TOK, COLS), lambda i: (i, 0, 0)),
            pl.BlockSpec((1, TOK, COLS), lambda i: (i, 0, 0)),
            pl.BlockSpec((TOK, 1), lambda i: (0, 0)),
        ],
        out_specs=pl.BlockSpec((TOK, 2 * COLS), lambda i: (0, i)),
        compiler_params=params(),
        cost_estimate=cost(0, 4 * TOK * D),
    )(core, own, other, probs)


def shards(grad_parts, master, moment, second, down_weight, tokens, routes, probs):
    core = lax.axis_index("c")
    low = lax.axis_index("xl")
    high = lax.axis_index("xh")
    core_id = core.reshape(1).astype(jnp.int32)
    group = ("z", "xl")

    grads = grad_parts.reshape(GROUP, C, ROWS, 128)
    sent = lax.dynamic_index_in_dim(grads, 1 - core, axis=1, keepdims=False)
    received = lax.ppermute(sent, "c", SWAP)

    down = down_weight[0]
    beside = lax.ppermute(down, "xh", SWAP)
    pair = jnp.where(
        high == 0, jnp.concatenate([down, beside], 1), jnp.concatenate([beside, down], 1)
    )
    beside = lax.ppermute(pair, "xl", SWAP)
    pair = jnp.where(low == 0, jnp.concatenate([pair, beside], 0), jnp.concatenate([beside, pair], 0))
    down_all = lax.all_gather(pair, ("z", "y"), axis=0, tiled=False).reshape(Z, Y, COLS, 128)

    packed = pack(tokens)
    chunk = add(core_id, grads, received, routes.reshape(1, TOK))
    arrived = lax.all_to_all(chunk, group, 0, 0, tiled=True)
    packed, arrived = lax.optimization_barrier((packed, arrived))
    columns = lax.all_to_all(packed, group, 0, 0, tiled=True)

    new_master, new_moment, short, route_all = adam(arrived, master[0], moment[0], second[0])
    pair_short = jnp.concatenate([short, lax.ppermute(short, "xh", SWAP)], axis=0)
    own = lax.all_gather(pair_short, "y", axis=0, tiled=True).reshape(EXPERTS, ROWS, 128)
    other = lax.ppermute(own, "c", SWAP)

    ids = jnp.stack([core, high]).astype(jnp.int32)
    parts = partial_sums(ids, own, other, columns, route_all)
    parts = lax.all_to_all(parts.reshape(GROUP, TOK, 128), group, 0, 0, tiled=True)
    hidden = hidden_units(parts, routes)
    beside = lax.ppermute(hidden, "c", SWAP)
    out_own, out_other = down_project(hidden, beside, down_all)
    out_other = lax.ppermute(out_other, "c", SWAP)
    mixed = mix(core_id, out_own, out_other, probs.reshape(TOK, 1))
    return new_master[None], new_moment[None], mixed


def solution(mesh):
    fine = Mesh(mesh.devices.reshape(Z, XL, C, Y, XH), ("z", "xl", "c", "y", "xh"))
    dp, expert = ("z", "xl", "c"), ("y", "xh")
    both = dp + expert
    in_specs = (
        P(expert, dp, None, None),
        P(expert, dp, None),
        P(expert, dp, None),
        P(expert, dp, None),
        P(expert, dp, None),
        P(both, None),
        P(both, None),
        P(both),
    )
    out_specs = (P(expert, dp, None), P(expert, dp, None), P(both, None))
    return jax.shard_map(shards, mesh=fine, in_specs=in_specs, out_specs=out_specs, check_vma=False)
```

```python
import functools

import jax
import jax.numpy as jnp
from jax import lax
from jax.experimental import pallas as pl
from jax.experimental.pallas import tpu as pltpu
from jax.sharding import Mesh, PartitionSpec as P

beta_one = 0.9
beta_two = 0.95
learn_rate = 0.005
decay_rate = 0.1
adam_eps = 1e-08
bias_one = 1.0 - 0.9**50
bias_two = 1.0 - 0.95**50

Z, XL, C, Y, XH = 8, 2, 2, 8, 2
GROUP = Z * XL
EXPERTS = Y * XH
D = 5120
ROWS = 160
COLS = 320
TOK = 128
UNITS = 64
SWAP = ((0, 1), (1, 0))

f32 = jnp.float32
bf16 = jnp.bfloat16


def params(mib):
    return pltpu.CompilerParams(vmem_limit_bytes=mib * 1024 * 1024)


def cost(flops, nbytes):
    return pl.CostEstimate(flops=flops, bytes_accessed=nbytes, transcendentals=0)


def pack_kernel(x_ref, o_ref):
    half = TOK // 2
    for k in range(o_ref.shape[0]):
        at = slice(k * COLS, (k + 1) * COLS)
        o_ref[k, :, :COLS] = x_ref[:half, at]
        o_ref[k, :, COLS:] = x_ref[half:, at]


def pack(tokens):
    steps = 2
    return pl.pallas_call(
        pack_kernel,
        out_shape=jax.ShapeDtypeStruct((GROUP, TOK // 2, 2 * COLS), bf16),
        grid=(steps,),
        in_specs=[pl.BlockSpec((TOK, D // steps), lambda i: (0, i))],
        out_specs=pl.BlockSpec((GROUP // steps, TOK // 2, 2 * COLS), lambda i: (i, 0, 0)),
        compiler_params=params(12),
        cost_estimate=cost(0, 2 * TOK * D * 2),
    )(tokens)


def add_kernel(c_ref, g_ref, r_ref, route_ref, o_ref):
    total = g_ref[:, 0].astype(f32) + r_ref[...].astype(f32)
    o_ref[:, :ROWS] = total.astype(bf16)
    rows = jnp.broadcast_to(route_ref[...].astype(f32), (16, TOK)).astype(bf16)
    for i in range(o_ref.shape[0]):
        o_ref[i, ROWS:] = rows


def add(core, grads, received, route_row):
    n = 8
    return pl.pallas_call(
        add_kernel,
        out_shape=jax.ShapeDtypeStruct((GROUP, ROWS + 16, TOK), bf16),
        grid_spec=pltpu.PrefetchScalarGridSpec(
            num_scalar_prefetch=1,
            grid=(GROUP // n,),
            in_specs=[
                pl.BlockSpec((n, 1, ROWS, 128), lambda i, c: (i, c[0], 0, 0)),
                pl.BlockSpec((n, ROWS, 128), lambda i, c: (i, 0, 0)),
                pl.BlockSpec((1, TOK), lambda i, c: (0, 0)),
            ],
            out_specs=pl.BlockSpec((n, ROWS + 16, TOK), lambda i, c: (i, 0, 0)),
        ),
        compiler_params=params(8),
        cost_estimate=cost(0, 3 * GROUP * ROWS * 256),
    )(core, grads, received, route_row)


def adam_kernel(g_ref, w_ref, m_ref, s_ref, nw_ref, nm_ref, short_ref, route_ref):
    total = g_ref[0, :ROWS].astype(f32)
    for i in range(1, GROUP):
        total = total + g_ref[i, :ROWS].astype(f32)
    weight = w_ref[...]
    moment_new = beta_one * m_ref[...] + (1.0 - beta_one) * total
    second_new = beta_two * s_ref[...] + (1.0 - beta_two) * total * total
    update = moment_new / bias_one / (jnp.sqrt(second_new / bias_two) + adam_eps)
    new_weight = weight - learn_rate * (update + decay_rate * weight)
    nw_ref[...] = new_weight
    nm_ref[...] = moment_new
    short_ref[...] = new_weight.astype(bf16)
    for i in range(GROUP):
        route_ref[i : i + 1, :] = g_ref[i, ROWS : ROWS + 16].astype(f32)[0:1]


def adam(arrived, master, moment, second):
    return pl.pallas_call(
        adam_kernel,
        out_shape=(
            jax.ShapeDtypeStruct((ROWS, 128), f32),
            jax.ShapeDtypeStruct((ROWS, 128), f32),
            jax.ShapeDtypeStruct((ROWS, 128), bf16),
            jax.ShapeDtypeStruct((GROUP, TOK), f32),
        ),
        compiler_params=params(8),
        cost_estimate=cost(0, GROUP * ROWS * 256 + 5 * ROWS * 512),
    )(arrived, master, moment, second)


def partial_kernel(ids_ref, own_ref, other_ref, x_ref, route_ref, o_ref, w_scr, x_scr, r_scr, sems):
    core = ids_ref[0]
    high = ids_ref[1]
    half = TOK // 2
    first = pltpu.make_async_copy(own_ref, w_scr.at[core], sems.at[0])
    second = pltpu.make_async_copy(other_ref, w_scr.at[1 - core], sems.at[1])
    first.start()
    second.start()
    columns = jnp.transpose(route_ref[...])
    for s in range(GROUP):
        x_scr[s * TOK : s * TOK + half, :] = x_ref[s, :, :COLS]
        x_scr[s * TOK + half : (s + 1) * TOK, :] = x_ref[s, :, COLS:]
        r_scr[s * TOK : (s + 1) * TOK, :] = jnp.broadcast_to(columns[:, s : s + 1], (TOK, 128)).astype(bf16)
    first.wait()
    second.wait()
    step = 1024

    def rows(i, carry):
        at = pl.ds(pl.multiple_of(i * step, step), step)
        kept = jnp.zeros((step, 128), bf16)
        route = r_scr[at, :]
        for e in range(0, EXPERTS, 2):
            weights = jnp.concatenate(
                [jnp.concatenate([w_scr[c, e], w_scr[c, e + 1]], axis=1) for c in range(C)], axis=0
            )
            both = jnp.dot(x_scr[at, :], weights, preferred_element_type=f32).astype(bf16)
            kept = jnp.where(route == (e + high).astype(f32).astype(bf16), both[:, :128], kept)
            kept = jnp.where(route == (e + 1 - high).astype(f32).astype(bf16), both[:, 128:], kept)
        o_ref[at, :] = kept
        return carry

    lax.fori_loop(0, GROUP * TOK // step, rows, 0)


def partial_sums(ids, own, other, x, route):
    vmem = pl.BlockSpec(memory_space=pltpu.VMEM)
    anywhere = pl.BlockSpec(memory_space=pl.ANY)
    return pl.pallas_call(
        partial_kernel,
        out_shape=jax.ShapeDtypeStruct((GROUP * TOK, 128), bf16),
        in_specs=[pl.BlockSpec(memory_space=pltpu.SMEM), anywhere, anywhere, vmem, vmem],
        out_specs=vmem,
        scratch_shapes=[
            pltpu.VMEM((C, EXPERTS, ROWS, 128), bf16),
            pltpu.VMEM((GROUP * TOK, COLS), bf16),
            pltpu.VMEM((GROUP * TOK, 128), bf16),
            pltpu.SemaphoreType.DMA((2,)),
        ],
        compiler_params=params(20),
        cost_estimate=cost(2 * GROUP * TOK * COLS * EXPERTS * 128, 4 * 1024 * 1024),
    )(ids, own, other, x, route)


def finish_kernel(p_ref, route_ref, prob_ref, d_ref, o_ref, w_scr, h_scr, prob_scr, sems):
    step = pl.program_id(0)
    n = Z // pl.num_programs(0)

    def weights(z):
        return pltpu.make_async_copy(d_ref.at[z], w_scr.at[z], sems.at[z])

    @pl.when(step == 0)
    def _():
        for z in range(Z):
            weights(z).start()
        total = p_ref[0].astype(f32)
        for i in range(1, GROUP):
            total = total + p_ref[i].astype(f32)
        gate = total[:, :UNITS]
        up = total[:, UNITS:]
        hidden = gate * jax.nn.sigmoid(gate) * up
        rows = [jnp.broadcast_to(r, (4, TOK)) for r in (route_ref[...].astype(f32), prob_ref[...])]
        columns = jnp.transpose(jnp.concatenate(rows, axis=0))
        route = jnp.broadcast_to(columns[:, 0:1], (TOK, UNITS))
        prob_scr[...] = jnp.broadcast_to(columns[:, 4:5], (TOK, 128))
        for j in range(XH):
            for y in range(Y):
                at = (j * Y + y) * UNITS
                h_scr[:, at : at + UNITS] = jnp.where(route == 2.0 * y + j, hidden, 0.0).astype(bf16)

    prob = jnp.concatenate([prob_scr[...]] * 5, axis=1)
    split = Y * UNITS
    for k in range(n):
        z = step * n + k
        weights(z).wait()
        outs = []
        for c in range(C):
            block = w_scr[z, :, c].reshape(split, 2 * COLS)
            low = jnp.dot(h_scr[:, :split], block[:, :COLS], preferred_element_type=f32)
            wide = jnp.dot(h_scr[:, split:], block[:, COLS - UNITS :], preferred_element_type=f32)
            outs.append((low + wide[:, UNITS:]).astype(bf16))
        even, odd = outs
        blocks = [even[:, :ROWS], odd[:, :ROWS], even[:, ROWS:], odd[:, ROWS:]]
        whole = jnp.concatenate(blocks, axis=1).astype(f32)
        o_ref[:, k * 2 * COLS : (k + 1) * 2 * COLS] = (prob * whole).astype(bf16)


def finish(parts, route_row, prob_row, down):
    steps = 4
    return pl.pallas_call(
        finish_kernel,
        out_shape=jax.ShapeDtypeStruct((TOK, D), bf16),
        grid=(steps,),
        in_specs=[
            pl.BlockSpec((GROUP, TOK, 128), lambda i: (0, 0, 0)),
            pl.BlockSpec((1, TOK), lambda i: (0, 0)),
            pl.BlockSpec((1, TOK), lambda i: (0, 0)),
            pl.BlockSpec(memory_space=pl.ANY),
        ],
        out_specs=pl.BlockSpec((TOK, D // steps), lambda i: (0, i)),
        scratch_shapes=[
            pltpu.VMEM((Z, Y, C, UNITS, 2 * COLS), bf16),
            pltpu.VMEM((TOK, EXPERTS * UNITS), bf16),
            pltpu.VMEM((TOK, 128), f32),
            pltpu.SemaphoreType.DMA((Z,)),
        ],
        compiler_params=params(52),
        cost_estimate=cost(2 * TOK * EXPERTS * UNITS * D, 12 * 1024 * 1024),
    )(parts, route_row, prob_row, down)


def shards(grad_parts, master, moment, second, down_weight, tokens, routes, probs):
    core = lax.axis_index("c")
    low = lax.axis_index("xl")
    high = lax.axis_index("xh")
    core_id = core.reshape(1).astype(jnp.int32)
    group = ("z", "xl")

    grads = grad_parts.reshape(GROUP, C, ROWS, 128)
    sent = lax.dynamic_index_in_dim(grads, 1 - core, axis=1, keepdims=False)
    received = lax.ppermute(sent, "c", SWAP)

    down = jnp.broadcast_to(down_weight[0].T[None], (XH * XL, UNITS, ROWS))
    four = lax.all_to_all(down, ("xh", "xl"), 0, 0, tiled=True)
    pair = jnp.transpose(four, (1, 0, 2)).reshape(UNITS, 2 * COLS)
    pair, received = lax.optimization_barrier((pair, received))
    down_all = lax.all_gather(pair, ("z", "y", "c"), axis=0, tiled=False)
    down_all = down_all.reshape(Z, Y, C, UNITS, 2 * COLS)
    chunk = add(core_id, grads, received, routes.reshape(1, TOK))
    arrived = lax.all_to_all(chunk, group, 0, 0, tiled=True)

    new_master, new_moment, short, route_all = adam(arrived, master[0], moment[0], second[0])
    pair_short = jnp.concatenate([short, lax.ppermute(short, "xh", SWAP)], axis=0)
    tokens, _ = lax.optimization_barrier((tokens, short))
    packed, pair_short = lax.optimization_barrier((pack(tokens), pair_short))
    columns = lax.all_to_all(packed, group, 0, 0, tiled=True)
    own = lax.all_gather(pair_short, "y", axis=0, tiled=True).reshape(EXPERTS, ROWS, 128)
    other = lax.ppermute(own, "c", SWAP)

    ids = jnp.stack([core, high]).astype(jnp.int32)
    parts = partial_sums(ids, own, other, columns, route_all)
    parts = lax.all_to_all(parts.reshape(GROUP, TOK, 128), group, 0, 0, tiled=True)
    mixed = finish(parts, routes.reshape(1, TOK), probs.reshape(1, TOK), down_all)
    return new_master[None], new_moment[None], mixed


def solution(mesh):
    fine = Mesh(mesh.devices.reshape(Z, XL, C, Y, XH), ("z", "xl", "c", "y", "xh"))
    dp, expert = ("z", "xl", "c"), ("y", "xh")
    both = dp + expert
    in_specs = (
        P(expert, dp, None, None),
        P(expert, dp, None),
        P(expert, dp, None),
        P(expert, dp, None),
        P(expert, dp, None),
        P(both, None),
        P(both, None),
        P(both),
    )
    out_specs = (P(expert, dp, None), P(expert, dp, None), P(both, None))
    return jax.shard_map(shards, mesh=fine, in_specs=in_specs, out_specs=out_specs, check_vma=False)
```

```python
import functools

import jax
import jax.numpy as jnp
from jax import lax
from jax.experimental import pallas as pl
from jax.experimental.pallas import tpu as pltpu
from jax.sharding import Mesh, PartitionSpec as P

beta_one = 0.9
beta_two = 0.95
learn_rate = 0.005
decay_rate = 0.1
adam_eps = 1e-08
bias_one = 1.0 - 0.9**50
bias_two = 1.0 - 0.95**50

Z, XL, C, Y, XH = 8, 2, 2, 8, 2
GROUP = Z * XL
EXPERTS = Y * XH
D = 5120
ROWS = 160
COLS = 320
TOK = 128
UNITS = 64
SWAP = ((0, 1), (1, 0))

f32 = jnp.float32
bf16 = jnp.bfloat16


def params(mib):
    return pltpu.CompilerParams(vmem_limit_bytes=mib * 1024 * 1024)


def cost(flops, nbytes):
    return pl.CostEstimate(flops=flops, bytes_accessed=nbytes, transcendentals=0)


def pack_kernel(x_ref, o_ref):
    quarter = TOK // 4
    for k in range(o_ref.shape[0]):
        for c in range(C):
            at = slice((k * C + c) * ROWS, (k * C + c + 1) * ROWS)
            part = x_ref[:, at]
            groups = [part[q * quarter : (q + 1) * quarter] for q in range(4)]
            o_ref[k, c] = jnp.concatenate(groups, axis=1)


def pack(tokens):
    steps = 2
    return pl.pallas_call(
        pack_kernel,
        out_shape=jax.ShapeDtypeStruct((GROUP, C, TOK // 4, 4 * ROWS), bf16),
        grid=(steps,),
        in_specs=[pl.BlockSpec((TOK, D // steps), lambda i: (0, i))],
        out_specs=pl.BlockSpec((GROUP // steps, C, TOK // 4, 4 * ROWS), lambda i: (i, 0, 0, 0)),
        compiler_params=params(12),
        cost_estimate=cost(0, 2 * TOK * D * 2),
    )(tokens)


def add_kernel(c_ref, g_ref, r_ref, route_ref, o_ref):
    total = g_ref[:, 0].astype(f32) + r_ref[...].astype(f32)
    o_ref[:, :ROWS] = total.astype(bf16)
    rows = jnp.broadcast_to(route_ref[...].astype(f32), (16, TOK)).astype(bf16)
    for i in range(o_ref.shape[0]):
        o_ref[i, ROWS:] = rows


def add(core, grads, received, route_row):
    n = 8
    return pl.pallas_call(
        add_kernel,
        out_shape=jax.ShapeDtypeStruct((GROUP, ROWS + 16, TOK), bf16),
        grid_spec=pltpu.PrefetchScalarGridSpec(
            num_scalar_prefetch=1,
            grid=(GROUP // n,),
            in_specs=[
                pl.BlockSpec((n, 1, ROWS, 128), lambda i, c: (i, c[0], 0, 0)),
                pl.BlockSpec((n, ROWS, 128), lambda i, c: (i, 0, 0)),
                pl.BlockSpec((1, TOK), lambda i, c: (0, 0)),
            ],
            out_specs=pl.BlockSpec((n, ROWS + 16, TOK), lambda i, c: (i, 0, 0)),
        ),
        compiler_params=params(8),
        cost_estimate=cost(0, 3 * GROUP * ROWS * 256),
    )(core, grads, received, route_row)


def adam_kernel(g_ref, w_ref, m_ref, s_ref, nw_ref, nm_ref, short_ref, route_ref):
    total = g_ref[0, :ROWS].astype(f32)
    for i in range(1, GROUP):
        total = total + g_ref[i, :ROWS].astype(f32)
    weight = w_ref[...]
    moment_new = beta_one * m_ref[...] + (1.0 - beta_one) * total
    second_new = beta_two * s_ref[...] + (1.0 - beta_two) * total * total
    update = moment_new / bias_one / (jnp.sqrt(second_new / bias_two) + adam_eps)
    new_weight = weight - learn_rate * (update + decay_rate * weight)
    nw_ref[...] = new_weight
    nm_ref[...] = moment_new
    short_ref[...] = new_weight.astype(bf16)
    for i in range(GROUP):
        route_ref[i : i + 1, :] = g_ref[i, ROWS : ROWS + 16].astype(f32)[0:1]


def adam(arrived, master, moment, second):
    return pl.pallas_call(
        adam_kernel,
        out_shape=(
            jax.ShapeDtypeStruct((ROWS, 128), f32),
            jax.ShapeDtypeStruct((ROWS, 128), f32),
            jax.ShapeDtypeStruct((ROWS, 128), bf16),
            jax.ShapeDtypeStruct((GROUP, TOK), f32),
        ),
        compiler_params=params(8),
        cost_estimate=cost(0, GROUP * ROWS * 256 + 5 * ROWS * 512),
    )(arrived, master, moment, second)


def select_sums(x_ref, core, w_ref, high, x_scr, route_ref, start, store):
    quarter = TOK // 4
    for s in range(GROUP):
        block = x_ref[s, core]
        for q in range(4):
            at = s * TOK + q * quarter
            x_scr[at : at + quarter, :] = block[:, q * ROWS : (q + 1) * ROWS]
    step = 1024

    def rows(i, carry):
        at = pl.ds(pl.multiple_of(i * step, step), step)
        kept = jnp.zeros((step, 128), f32)
        route = route_ref[at, :].astype(f32)
        for e in range(0, EXPERTS, 2):
            weights = jnp.concatenate([w_ref[e], w_ref[e + 1]], axis=1)
            both = jnp.dot(x_scr[at, :], weights, preferred_element_type=f32)
            kept = jnp.where(route == (e + high).astype(f32), both[:, :128], kept)
            kept = jnp.where(route == (e + 1 - high).astype(f32), both[:, 128:], kept)
        store(at, kept if start is None else kept + start[at, :])
        return carry

    lax.fori_loop(0, GROUP * TOK // step, rows, 0)


def first_kernel(ids_ref, w_ref, x_ref, route_ref, o_ref, spread_ref, x_scr):
    columns = jnp.transpose(route_ref[...])
    for s in range(GROUP):
        wide = jnp.broadcast_to(columns[:, s : s + 1], (TOK, 128))
        spread_ref[s * TOK : (s + 1) * TOK, :] = wide.astype(bf16)

    def store(at, value):
        o_ref[at, :] = value

    select_sums(x_ref, ids_ref[0], w_ref, ids_ref[1], x_scr, spread_ref, None, store)


def second_kernel(ids_ref, w_ref, x_ref, spread_ref, p_ref, o_ref, x_scr):
    def store(at, value):
        o_ref[at, :] = value.astype(bf16)

    select_sums(x_ref, 1 - ids_ref[0], w_ref, ids_ref[1], x_scr, spread_ref, p_ref, store)


def first_sums(ids, weights, x, route):
    vmem = pl.BlockSpec(memory_space=pltpu.VMEM)
    return pl.pallas_call(
        first_kernel,
        out_shape=(
            jax.ShapeDtypeStruct((GROUP * TOK, 128), f32),
            jax.ShapeDtypeStruct((GROUP * TOK, 128), bf16),
        ),
        in_specs=[pl.BlockSpec(memory_space=pltpu.SMEM), vmem, vmem, vmem],
        out_specs=(vmem, vmem),
        scratch_shapes=[pltpu.VMEM((GROUP * TOK, ROWS), bf16)],
        compiler_params=params(20),
        cost_estimate=cost(2 * GROUP * TOK * ROWS * EXPERTS * 128, 4 * 1024 * 1024),
    )(ids, weights, x, route)


def second_sums(ids, weights, x, spread, parts):
    vmem = pl.BlockSpec(memory_space=pltpu.VMEM)
    return pl.pallas_call(
        second_kernel,
        out_shape=jax.ShapeDtypeStruct((GROUP * TOK, 128), bf16),
        in_specs=[pl.BlockSpec(memory_space=pltpu.SMEM)] + [vmem] * 4,
        out_specs=vmem,
        scratch_shapes=[pltpu.VMEM((GROUP * TOK, ROWS), bf16)],
        compiler_params=params(20),
        cost_estimate=cost(2 * GROUP * TOK * ROWS * EXPERTS * 128, 4 * 1024 * 1024),
    )(ids, weights, x, spread, parts)


def finish_kernel(p_ref, route_ref, prob_ref, d_ref, o_ref, w_scr, h_scr, prob_scr, sems):
    step = pl.program_id(0)
    n = Z // pl.num_programs(0)

    def weights(z):
        return pltpu.make_async_copy(d_ref.at[z], w_scr.at[z], sems.at[z])

    @pl.when(step == 0)
    def _():
        for z in range(Z):
            weights(z).start()
        total = p_ref[0].astype(f32)
        for i in range(1, GROUP):
            total = total + p_ref[i].astype(f32)
        gate = total[:, :UNITS]
        up = total[:, UNITS:]
        hidden = gate * jax.nn.sigmoid(gate) * up
        rows = [jnp.broadcast_to(r, (4, TOK)) for r in (route_ref[...].astype(f32), prob_ref[...])]
        columns = jnp.transpose(jnp.concatenate(rows, axis=0))
        route = jnp.broadcast_to(columns[:, 0:1], (TOK, UNITS))
        prob_scr[...] = jnp.broadcast_to(columns[:, 4:5], (TOK, 128))
        for j in range(XH):
            for y in range(Y):
                at = (j * Y + y) * UNITS
                h_scr[:, at : at + UNITS] = jnp.where(route == 2.0 * y + j, hidden, 0.0).astype(bf16)

    prob = jnp.concatenate([prob_scr[...]] * 5, axis=1)
    split = Y * UNITS
    for k in range(n):
        z = step * n + k
        weights(z).wait()
        outs = []
        for c in range(C):
            block = w_scr[z, :, c].reshape(split, 2 * COLS)
            low = jnp.dot(h_scr[:, :split], block[:, :COLS], preferred_element_type=f32)
            wide = jnp.dot(h_scr[:, split:], block[:, COLS - UNITS :], preferred_element_type=f32)
            outs.append((low + wide[:, UNITS:]).astype(bf16))
        even, odd = outs
        blocks = [even[:, :ROWS], odd[:, :ROWS], even[:, ROWS:], odd[:, ROWS:]]
        whole = jnp.concatenate(blocks, axis=1).astype(f32)
        o_ref[:, k * 2 * COLS : (k + 1) * 2 * COLS] = (prob * whole).astype(bf16)


def finish(parts, route_row, prob_row, down):
    steps = 4
    return pl.pallas_call(
        finish_kernel,
        out_shape=jax.ShapeDtypeStruct((TOK, D), bf16),
        grid=(steps,),
        in_specs=[
            pl.BlockSpec((GROUP, TOK, 128), lambda i: (0, 0, 0)),
            pl.BlockSpec((1, TOK), lambda i: (0, 0)),
            pl.BlockSpec((1, TOK), lambda i: (0, 0)),
            pl.BlockSpec(memory_space=pl.ANY),
        ],
        out_specs=pl.BlockSpec((TOK, D // steps), lambda i: (0, i)),
        scratch_shapes=[
            pltpu.VMEM((Z, Y, C, UNITS, 2 * COLS), bf16),
            pltpu.VMEM((TOK, EXPERTS * UNITS), bf16),
            pltpu.VMEM((TOK, 128), f32),
            pltpu.SemaphoreType.DMA((Z,)),
        ],
        compiler_params=params(52),
        cost_estimate=cost(2 * TOK * EXPERTS * UNITS * D, 12 * 1024 * 1024),
    )(parts, route_row, prob_row, down)


def shards(grad_parts, master, moment, second, down_weight, tokens, routes, probs):
    core = lax.axis_index("c")
    low = lax.axis_index("xl")
    high = lax.axis_index("xh")
    core_id = core.reshape(1).astype(jnp.int32)
    group = ("z", "xl")

    grads = grad_parts.reshape(GROUP, C, ROWS, 128)
    sent = lax.dynamic_index_in_dim(grads, 1 - core, axis=1, keepdims=False)
    received = lax.ppermute(sent, "c", SWAP)

    down = jnp.broadcast_to(down_weight[0].T[None], (XH * XL, UNITS, ROWS))
    four = lax.all_to_all(down, ("xh", "xl"), 0, 0, tiled=True)
    pair = jnp.transpose(four, (1, 0, 2)).reshape(UNITS, 2 * COLS)
    pair, received = lax.optimization_barrier((pair, received))
    down_all = lax.all_gather(pair, ("z", "y", "c"), axis=0, tiled=False)
    down_all = down_all.reshape(Z, Y, C, UNITS, 2 * COLS)
    chunk = add(core_id, grads, received, routes.reshape(1, TOK))
    arrived = lax.all_to_all(chunk, group, 0, 0, tiled=True)
    packed, arrived = lax.optimization_barrier((pack(tokens), arrived))
    columns = lax.all_to_all(packed, group, 0, 0, tiled=True)

    new_master, new_moment, short, route_all = adam(arrived, master[0], moment[0], second[0])
    pair_short = jnp.concatenate([short, lax.ppermute(short, "xh", SWAP)], axis=0)
    own = lax.all_gather(pair_short, "y", axis=0, tiled=True).reshape(EXPERTS, ROWS, 128)
    other = lax.ppermute(own, "c", SWAP)

    ids = jnp.stack([core, high]).astype(jnp.int32)
    parts, spread = first_sums(ids, own, columns, route_all)
    parts = second_sums(ids, other, columns, spread, parts)
    parts = lax.all_to_all(parts.reshape(GROUP, TOK, 128), group, 0, 0, tiled=True)
    mixed = finish(parts, routes.reshape(1, TOK), probs.reshape(1, TOK), down_all)
    return new_master[None], new_moment[None], mixed


def solution(mesh):
    fine = Mesh(mesh.devices.reshape(Z, XL, C, Y, XH), ("z", "xl", "c", "y", "xh"))
    dp, expert = ("z", "xl", "c"), ("y", "xh")
    both = dp + expert
    in_specs = (
        P(expert, dp, None, None),
        P(expert, dp, None),
        P(expert, dp, None),
        P(expert, dp, None),
        P(expert, dp, None),
        P(both, None),
        P(both, None),
        P(both),
    )
    out_specs = (P(expert, dp, None), P(expert, dp, None), P(both, None))
    return jax.shard_map(shards, mesh=fine, in_specs=in_specs, out_specs=out_specs, check_vma=False)
```

```python
import functools

import jax
import jax.numpy as jnp
from jax import lax
from jax.experimental import pallas as pl
from jax.experimental.pallas import tpu as pltpu
from jax.sharding import Mesh, PartitionSpec as P

beta_one = 0.9
beta_two = 0.95
learn_rate = 0.005
decay_rate = 0.1
adam_eps = 1e-08
bias_one = 1.0 - 0.9**50
bias_two = 1.0 - 0.95**50

Z, XL, C, Y, XH = 8, 2, 2, 8, 2
GROUP = Z * XL
EXPERTS = Y * XH
D = 5120
ROWS = 160
COLS = 320
TOK = 128
UNITS = 64
SWAP = ((0, 1), (1, 0))

f32 = jnp.float32
bf16 = jnp.bfloat16


def params(mib):
    return pltpu.CompilerParams(vmem_limit_bytes=mib * 1024 * 1024)


def cost(flops, nbytes):
    return pl.CostEstimate(flops=flops, bytes_accessed=nbytes, transcendentals=0)


def pack_kernel(x_ref, o_ref):
    quarter = TOK // 4
    for k in range(o_ref.shape[0]):
        for c in range(C):
            at = (k * C + c) * ROWS
            part = x_ref[:, at : at + ROWS]
            groups = [part[q * quarter : (q + 1) * quarter] for q in range(4)]
            wide = [g[:, :128] for g in groups]
            rest = [g[:, 128:] for g in groups]
            o_ref[k, c] = jnp.concatenate(wide + rest, axis=1)


def pack(tokens):
    steps = 2
    return pl.pallas_call(
        pack_kernel,
        out_shape=jax.ShapeDtypeStruct((GROUP, C, TOK // 4, 4 * ROWS), bf16),
        grid=(steps,),
        in_specs=[pl.BlockSpec((TOK, D // steps), lambda i: (0, i))],
        out_specs=pl.BlockSpec((GROUP // steps, C, TOK // 4, 4 * ROWS), lambda i: (i, 0, 0, 0)),
        compiler_params=params(12),
        cost_estimate=cost(0, 2 * TOK * D * 2),
    )(tokens)


def add_kernel(c_ref, g_ref, r_ref, route_ref, o_ref):
    total = g_ref[:, 0].astype(f32) + r_ref[...].astype(f32)
    o_ref[:, :ROWS] = total.astype(bf16)
    rows = jnp.broadcast_to(route_ref[...].astype(f32), (16, TOK)).astype(bf16)
    for i in range(o_ref.shape[0]):
        o_ref[i, ROWS:] = rows


def add(core, grads, received, route_row):
    n = 8
    return pl.pallas_call(
        add_kernel,
        out_shape=jax.ShapeDtypeStruct((GROUP, ROWS + 16, TOK), bf16),
        grid_spec=pltpu.PrefetchScalarGridSpec(
            num_scalar_prefetch=1,
            grid=(GROUP // n,),
            in_specs=[
                pl.BlockSpec((n, 1, ROWS, 128), lambda i, c: (i, c[0], 0, 0)),
                pl.BlockSpec((n, ROWS, 128), lambda i, c: (i, 0, 0)),
                pl.BlockSpec((1, TOK), lambda i, c: (0, 0)),
            ],
            out_specs=pl.BlockSpec((n, ROWS + 16, TOK), lambda i, c: (i, 0, 0)),
        ),
        compiler_params=params(8),
        cost_estimate=cost(0, 3 * GROUP * ROWS * 256),
    )(core, grads, received, route_row)


def adam_kernel(g_ref, w_ref, m_ref, s_ref, nw_ref, nm_ref, short_ref, route_ref):
    total = g_ref[0, :ROWS].astype(f32)
    for i in range(1, GROUP):
        total = total + g_ref[i, :ROWS].astype(f32)
    weight = w_ref[...]
    moment_new = beta_one * m_ref[...] + (1.0 - beta_one) * total
    second_new = beta_two * s_ref[...] + (1.0 - beta_two) * total * total
    update = moment_new / bias_one / (jnp.sqrt(second_new / bias_two) + adam_eps)
    new_weight = weight - learn_rate * (update + decay_rate * weight)
    nw_ref[...] = new_weight
    nm_ref[...] = moment_new
    short_ref[...] = new_weight.astype(bf16)
    for i in range(GROUP):
        route_ref[i : i + 1, :] = g_ref[i, ROWS : ROWS + 16].astype(f32)[0:1]


def adam(arrived, master, moment, second):
    return pl.pallas_call(
        adam_kernel,
        out_shape=(
            jax.ShapeDtypeStruct((ROWS, 128), f32),
            jax.ShapeDtypeStruct((ROWS, 128), f32),
            jax.ShapeDtypeStruct((ROWS, 128), bf16),
            jax.ShapeDtypeStruct((GROUP, TOK), f32),
        ),
        compiler_params=params(8),
        cost_estimate=cost(0, GROUP * ROWS * 256 + 5 * ROWS * 512),
    )(arrived, master, moment, second)


def select_sums(x_ref, core, w_ref, x_scr, y_scr, place_ref, start, store):
    quarter = TOK // 4
    lane = lax.broadcasted_iota(jnp.int32, (quarter, 128), 1)
    for s in range(GROUP):
        block = x_ref[s, core]
        rest = block[:, 512:].astype(f32)
        turned = [rest] + [
            jnp.concatenate([rest[:, 128 - 32 * k :], rest[:, : 128 - 32 * k]], axis=1)
            for k in range(1, 4)
        ]
        for q in range(4):
            at = slice(s * TOK + q * quarter, s * TOK + (q + 1) * quarter)
            x_scr[at, :] = block[:, 128 * q : 128 * (q + 1)]
            spread = turned[(3 - q) % 4]
            for g in range(3):
                spread = jnp.where((lane >= 32 * g) & (lane < 32 * (g + 1)), turned[(g - q) % 4], spread)
            y_scr[at, :] = spread.astype(bf16)
    half = EXPERTS // 2
    rows_of = [jnp.concatenate([w_ref[j, :128], w_ref[j + half, :128]], axis=1) for j in range(half)]
    rows_of += [jnp.concatenate([w_ref[j, 128:], w_ref[j + half, 128:]], axis=1) for j in range(half)]
    weights = jnp.concatenate(rows_of, axis=0)
    step = 512

    def rows(i, carry):
        at = pl.ds(pl.multiple_of(i * step, step), step)
        place = place_ref[at, :]
        group = (lax.broadcasted_iota(jnp.int32, (step, 128), 1) // 32).astype(f32).astype(bf16)
        eight = jnp.asarray(half, bf16)
        within = jnp.where(place >= eight, place - eight, place)
        x = x_scr[at, :]
        y = y_scr[at, :]
        none = jnp.zeros((step, 128), bf16)
        copies = [jnp.where(within == jnp.asarray(j, bf16), x, none) for j in range(half)]
        copies += [jnp.where(within == group + jnp.asarray(4 * h, bf16), y, none) for h in range(2)]
        both = jnp.dot(jnp.concatenate(copies, axis=1), weights, preferred_element_type=f32)
        kept = jnp.where(place.astype(f32) >= float(half), both[:, 128:], both[:, :128])
        store(at, kept if start is None else kept + start[at, :])
        return carry

    lax.fori_loop(0, GROUP * TOK // step, rows, 0, unroll=True)


def first_kernel(ids_ref, w_ref, x_ref, route_ref, o_ref, place_ref, x_scr, y_scr):
    route = route_ref[...]
    low_bit = route - 2.0 * jnp.floor(route * 0.5)
    columns = jnp.transpose(jnp.where(ids_ref[1] == 0, route, route + 1.0 - 2.0 * low_bit))
    for s in range(GROUP):
        wide = jnp.broadcast_to(columns[:, s : s + 1], (TOK, 128))
        place_ref[s * TOK : (s + 1) * TOK, :] = wide.astype(bf16)

    def store(at, value):
        o_ref[at, :] = value

    select_sums(x_ref, ids_ref[0], w_ref, x_scr, y_scr, place_ref, None, store)


def second_kernel(ids_ref, w_ref, x_ref, place_ref, p_ref, o_ref, x_scr, y_scr):
    def store(at, value):
        o_ref[at, :] = value.astype(bf16)

    select_sums(x_ref, 1 - ids_ref[0], w_ref, x_scr, y_scr, place_ref, p_ref, store)


def first_sums(ids, weights, x, route):
    vmem = pl.BlockSpec(memory_space=pltpu.VMEM)
    return pl.pallas_call(
        first_kernel,
        out_shape=(
            jax.ShapeDtypeStruct((GROUP * TOK, 128), f32),
            jax.ShapeDtypeStruct((GROUP * TOK, 128), bf16),
        ),
        in_specs=[pl.BlockSpec(memory_space=pltpu.SMEM), vmem, vmem, vmem],
        out_specs=(vmem, vmem),
        scratch_shapes=[pltpu.VMEM((GROUP * TOK, 128), bf16)] * 2,
        compiler_params=params(20),
        cost_estimate=cost(2 * GROUP * TOK * ROWS * EXPERTS * 128, 4 * 1024 * 1024),
    )(ids, weights, x, route)


def second_sums(ids, weights, x, place, parts):
    vmem = pl.BlockSpec(memory_space=pltpu.VMEM)
    return pl.pallas_call(
        second_kernel,
        out_shape=jax.ShapeDtypeStruct((GROUP * TOK, 128), bf16),
        in_specs=[pl.BlockSpec(memory_space=pltpu.SMEM)] + [vmem] * 4,
        out_specs=vmem,
        scratch_shapes=[pltpu.VMEM((GROUP * TOK, 128), bf16)] * 2,
        compiler_params=params(20),
        cost_estimate=cost(2 * GROUP * TOK * ROWS * EXPERTS * 128, 4 * 1024 * 1024),
    )(ids, weights, x, place, parts)


def finish_kernel(p_ref, route_ref, prob_ref, d_ref, o_ref, w_scr, h_scr, prob_scr, sems):
    step = pl.program_id(0)
    n = Z // pl.num_programs(0)

    def weights(z):
        return pltpu.make_async_copy(d_ref.at[z], w_scr.at[z], sems.at[z])

    @pl.when(step == 0)
    def _():
        for z in range(Z):
            weights(z).start()
        total = p_ref[0].astype(f32)
        for i in range(1, GROUP):
            total = total + p_ref[i].astype(f32)
        gate = total[:, :UNITS]
        up = total[:, UNITS:]
        hidden = gate * jax.nn.sigmoid(gate) * up
        rows = [jnp.broadcast_to(r, (4, TOK)) for r in (route_ref[...].astype(f32), prob_ref[...])]
        columns = jnp.transpose(jnp.concatenate(rows, axis=0))
        route = jnp.broadcast_to(columns[:, 0:1], (TOK, UNITS))
        prob_scr[...] = jnp.broadcast_to(columns[:, 4:5], (TOK, 128))
        for j in range(XH):
            for y in range(Y):
                at = (j * Y + y) * UNITS
                h_scr[:, at : at + UNITS] = jnp.where(route == 2.0 * y + j, hidden, 0.0).astype(bf16)

    prob = jnp.concatenate([prob_scr[...]] * 5, axis=1)
    split = Y * UNITS
    lane = lax.broadcasted_iota(jnp.int32, (split, 128), 1)

    def beside(left, right):
        middle = jnp.where(lane < UNITS, left[:, 256:384].astype(f32), right[:, 256:384].astype(f32))
        return jnp.concatenate([left[:, :256], middle.astype(bf16), right[:, 384:]], axis=1)

    for k in range(n):
        z = step * n + k
        weights(z).wait()
        even = w_scr[z, :, 0].reshape(split, 2 * COLS)
        odd = w_scr[z, :, 1].reshape(split, 2 * COLS)
        low = jnp.dot(h_scr[:, :split], beside(even, odd), preferred_element_type=f32)
        high = jnp.dot(h_scr[:, split:], beside(odd, even), preferred_element_type=f32)
        total = low + jnp.concatenate([high[:, COLS:], high[:, :COLS]], axis=1)
        total = total.astype(bf16)
        blocks = [total[:, i * ROWS : (i + 1) * ROWS] for i in (0, 2, 1, 3)]
        whole = jnp.concatenate(blocks, axis=1).astype(f32)
        o_ref[:, k * 2 * COLS : (k + 1) * 2 * COLS] = (prob * whole).astype(bf16)


def finish(parts, route_row, prob_row, down):
    steps = 4
    return pl.pallas_call(
        finish_kernel,
        out_shape=jax.ShapeDtypeStruct((TOK, D), bf16),
        grid=(steps,),
        in_specs=[
            pl.BlockSpec((GROUP, TOK, 128), lambda i: (0, 0, 0)),
            pl.BlockSpec((1, TOK), lambda i: (0, 0)),
            pl.BlockSpec((1, TOK), lambda i: (0, 0)),
            pl.BlockSpec(memory_space=pl.ANY),
        ],
        out_specs=pl.BlockSpec((TOK, D // steps), lambda i: (0, i)),
        scratch_shapes=[
            pltpu.VMEM((Z, Y, C, UNITS, 2 * COLS), bf16),
            pltpu.VMEM((TOK, EXPERTS * UNITS), bf16),
            pltpu.VMEM((TOK, 128), f32),
            pltpu.SemaphoreType.DMA((Z,)),
        ],
        compiler_params=params(52),
        cost_estimate=cost(2 * TOK * EXPERTS * UNITS * D, 12 * 1024 * 1024),
    )(parts, route_row, prob_row, down)


def shards(grad_parts, master, moment, second, down_weight, tokens, routes, probs):
    core = lax.axis_index("c")
    low = lax.axis_index("xl")
    high = lax.axis_index("xh")
    core_id = core.reshape(1).astype(jnp.int32)
    group = ("z", "xl")

    grads = grad_parts.reshape(GROUP, C, ROWS, 128)
    sent = lax.dynamic_index_in_dim(grads, 1 - core, axis=1, keepdims=False)
    received = lax.ppermute(sent, "c", SWAP)

    down = jnp.broadcast_to(down_weight[0].T[None], (XH * XL, UNITS, ROWS))
    four = lax.all_to_all(down, ("xh", "xl"), 0, 0, tiled=True)
    pair = jnp.transpose(four, (1, 0, 2)).reshape(UNITS, 2 * COLS)
    pair = jnp.where(core == 0, pair, jnp.concatenate([pair[:, COLS:], pair[:, :COLS]], 1))
    pair, received = lax.optimization_barrier((pair, received))
    down_all = lax.all_gather(pair, ("z", "y", "c"), axis=0, tiled=False)
    down_all = down_all.reshape(Z, Y, C, UNITS, 2 * COLS)
    chunk = add(core_id, grads, received, routes.reshape(1, TOK))
    arrived = lax.all_to_all(chunk, group, 0, 0, tiled=True)
    packed, arrived = lax.optimization_barrier((pack(tokens), arrived))
    columns = lax.all_to_all(packed, group, 0, 0, tiled=True)

    new_master, new_moment, short, route_all = adam(arrived, master[0], moment[0], second[0])
    pair_short = jnp.concatenate([short, lax.ppermute(short, "xh", SWAP)], axis=0)
    own = lax.all_gather(pair_short, "y", axis=0, tiled=True).reshape(EXPERTS, ROWS, 128)
    other = lax.ppermute(own, "c", SWAP)

    ids = jnp.stack([core, high]).astype(jnp.int32)
    parts, place = first_sums(ids, own, columns, route_all)
    parts = second_sums(ids, other, columns, place, parts)
    parts = lax.all_to_all(parts.reshape(GROUP, TOK, 128), group, 0, 0, tiled=True)
    mixed = finish(parts, routes.reshape(1, TOK), probs.reshape(1, TOK), down_all)
    return new_master[None], new_moment[None], mixed


def solution(mesh):
    fine = Mesh(mesh.devices.reshape(Z, XL, C, Y, XH), ("z", "xl", "c", "y", "xh"))
    dp, expert = ("z", "xl", "c"), ("y", "xh")
    both = dp + expert
    in_specs = (
        P(expert, dp, None, None),
        P(expert, dp, None),
        P(expert, dp, None),
        P(expert, dp, None),
        P(expert, dp, None),
        P(both, None),
        P(both, None),
        P(both),
    )
    out_specs = (P(expert, dp, None), P(expert, dp, None), P(both, None))
    return jax.shard_map(shards, mesh=fine, in_specs=in_specs, out_specs=out_specs, check_vma=False)
```

```python
import functools

import jax
import jax.numpy as jnp
from jax import lax
from jax.experimental import pallas as pl
from jax.experimental.pallas import tpu as pltpu
from jax.sharding import Mesh, PartitionSpec as P

beta_one = 0.9
beta_two = 0.95
learn_rate = 0.005
decay_rate = 0.1
adam_eps = 1e-08
bias_one = 1.0 - 0.9**50
bias_two = 1.0 - 0.95**50

Z, XL, C, Y, XH = 8, 2, 2, 8, 2
GROUP = Z * XL
EXPERTS = Y * XH
D = 5120
ROWS = 160
COLS = 320
TOK = 128
UNITS = 64
SWAP = ((0, 1), (1, 0))

f32 = jnp.float32
bf16 = jnp.bfloat16


def params(mib):
    return pltpu.CompilerParams(vmem_limit_bytes=mib * 1024 * 1024)


def cost(flops, nbytes):
    return pl.CostEstimate(flops=flops, bytes_accessed=nbytes, transcendentals=0)


def pack_kernel(x_ref, o_ref):
    quarter = TOK // 4
    for k in range(o_ref.shape[0]):
        for c in range(C):
            at = (k * C + c) * ROWS
            part = x_ref[:, at : at + ROWS]
            groups = [part[q * quarter : (q + 1) * quarter] for q in range(4)]
            wide = [g[:, :128] for g in groups]
            rest = [g[:, 128:] for g in groups]
            o_ref[k, c] = jnp.concatenate(wide + rest, axis=1)


def pack(tokens):
    steps = 2
    return pl.pallas_call(
        pack_kernel,
        out_shape=jax.ShapeDtypeStruct((GROUP, C, TOK // 4, 4 * ROWS), bf16),
        grid=(steps,),
        in_specs=[pl.BlockSpec((TOK, D // steps), lambda i: (0, i))],
        out_specs=pl.BlockSpec((GROUP // steps, C, TOK // 4, 4 * ROWS), lambda i: (i, 0, 0, 0)),
        compiler_params=params(12),
        cost_estimate=cost(0, 2 * TOK * D * 2),
    )(tokens)


def add_kernel(c_ref, g_ref, r_ref, route_ref, o_ref):
    total = g_ref[:, 0].astype(f32) + r_ref[...].astype(f32)
    o_ref[:, :ROWS] = total.astype(bf16)
    rows = jnp.broadcast_to(route_ref[...].astype(f32), (16, TOK)).astype(bf16)
    for i in range(o_ref.shape[0]):
        o_ref[i, ROWS:] = rows


def add(core, grads, received, route_row):
    n = 8
    return pl.pallas_call(
        add_kernel,
        out_shape=jax.ShapeDtypeStruct((GROUP, ROWS + 16, TOK), bf16),
        grid_spec=pltpu.PrefetchScalarGridSpec(
            num_scalar_prefetch=1,
            grid=(GROUP // n,),
            in_specs=[
                pl.BlockSpec((n, 1, ROWS, 128), lambda i, c: (i, c[0], 0, 0)),
                pl.BlockSpec((n, ROWS, 128), lambda i, c: (i, 0, 0)),
                pl.BlockSpec((1, TOK), lambda i, c: (0, 0)),
            ],
            out_specs=pl.BlockSpec((n, ROWS + 16, TOK), lambda i, c: (i, 0, 0)),
        ),
        compiler_params=params(8),
        cost_estimate=cost(0, 3 * GROUP * ROWS * 256),
    )(core, grads, received, route_row)


def adam_kernel(g_ref, w_ref, m_ref, s_ref, nw_ref, nm_ref, short_ref, route_ref):
    total = g_ref[0, :ROWS].astype(f32)
    for i in range(1, GROUP):
        total = total + g_ref[i, :ROWS].astype(f32)
    weight = w_ref[...]
    moment_new = beta_one * m_ref[...] + (1.0 - beta_one) * total
    second_new = beta_two * s_ref[...] + (1.0 - beta_two) * total * total
    update = moment_new / bias_one / (jnp.sqrt(second_new / bias_two) + adam_eps)
    new_weight = weight - learn_rate * (update + decay_rate * weight)
    nw_ref[...] = new_weight
    nm_ref[...] = moment_new
    short_ref[...] = new_weight.astype(bf16)
    for i in range(GROUP):
        route_ref[i : i + 1, :] = g_ref[i, ROWS : ROWS + 16].astype(f32)[0:1]


def adam(arrived, master, moment, second):
    return pl.pallas_call(
        adam_kernel,
        out_shape=(
            jax.ShapeDtypeStruct((ROWS, 128), f32),
            jax.ShapeDtypeStruct((ROWS, 128), f32),
            jax.ShapeDtypeStruct((ROWS, 128), bf16),
            jax.ShapeDtypeStruct((GROUP, TOK), f32),
        ),
        compiler_params=params(8),
        cost_estimate=cost(0, GROUP * ROWS * 256 + 5 * ROWS * 512),
    )(arrived, master, moment, second)


def select_sums(x_ref, core, w_ref, x_scr, y_scr, place_ref, start, store):
    quarter = TOK // 4
    lane = lax.broadcasted_iota(jnp.int32, (quarter, 128), 1)
    for s in range(GROUP):
        block = x_ref[s, core]
        rest = block[:, 512:].astype(f32)
        turned = [rest] + [
            jnp.concatenate([rest[:, 128 - 32 * k :], rest[:, : 128 - 32 * k]], axis=1)
            for k in range(1, 4)
        ]
        for q in range(4):
            at = slice(s * TOK + q * quarter, s * TOK + (q + 1) * quarter)
            x_scr[at, :] = block[:, 128 * q : 128 * (q + 1)]
            spread = turned[(3 - q) % 4]
            for g in range(3):
                spread = jnp.where((lane >= 32 * g) & (lane < 32 * (g + 1)), turned[(g - q) % 4], spread)
            y_scr[at, :] = spread.astype(bf16)
    half = EXPERTS // 2
    rows_of = [jnp.concatenate([w_ref[j, :128], w_ref[j + half, :128]], axis=1) for j in range(half)]
    rows_of += [jnp.concatenate([w_ref[j, 128:], w_ref[j + half, 128:]], axis=1) for j in range(half)]
    weights = jnp.concatenate(rows_of, axis=0)
    step = 512

    def rows(i, carry):
        at = pl.ds(pl.multiple_of(i * step, step), step)
        place = place_ref[at, :]
        group = (lax.broadcasted_iota(jnp.int32, (step, 128), 1) // 32).astype(f32).astype(bf16)
        eight = jnp.asarray(half, bf16)
        within = jnp.where(place >= eight, place - eight, place)
        x = x_scr[at, :]
        y = y_scr[at, :]
        none = jnp.zeros((step, 128), bf16)
        copies = [jnp.where(within == jnp.asarray(j, bf16), x, none) for j in range(half)]
        copies += [jnp.where(within == group + jnp.asarray(4 * h, bf16), y, none) for h in range(2)]
        both = jnp.dot(jnp.concatenate(copies, axis=1), weights, preferred_element_type=f32)
        kept = jnp.where(place.astype(f32) >= float(half), both[:, 128:], both[:, :128])
        store(at, kept if start is None else kept + start[at, :])
        return carry

    lax.fori_loop(0, GROUP * TOK // step, rows, 0, unroll=True)


def first_kernel(ids_ref, w_ref, x_ref, route_ref, o_ref, place_ref, x_scr, y_scr):
    route = route_ref[...]
    low_bit = route - 2.0 * jnp.floor(route * 0.5)
    columns = jnp.transpose(jnp.where(ids_ref[1] == 0, route, route + 1.0 - 2.0 * low_bit))
    for s in range(GROUP):
        wide = jnp.broadcast_to(columns[:, s : s + 1], (TOK, 128))
        place_ref[s * TOK : (s + 1) * TOK, :] = wide.astype(bf16)

    def store(at, value):
        o_ref[at, :] = value

    select_sums(x_ref, ids_ref[0], w_ref, x_scr, y_scr, place_ref, None, store)


def second_kernel(ids_ref, w_ref, x_ref, place_ref, p_ref, o_ref, x_scr, y_scr):
    def store(at, value):
        o_ref[at, :] = value.astype(bf16)

    select_sums(x_ref, 1 - ids_ref[0], w_ref, x_scr, y_scr, place_ref, p_ref, store)


def first_sums(ids, weights, x, route):
    vmem = pl.BlockSpec(memory_space=pltpu.VMEM)
    return pl.pallas_call(
        first_kernel,
        out_shape=(
            jax.ShapeDtypeStruct((GROUP * TOK, 128), f32),
            jax.ShapeDtypeStruct((GROUP * TOK, 128), bf16),
        ),
        in_specs=[pl.BlockSpec(memory_space=pltpu.SMEM), vmem, vmem, vmem],
        out_specs=(vmem, vmem),
        scratch_shapes=[pltpu.VMEM((GROUP * TOK, 128), bf16)] * 2,
        compiler_params=params(20),
        cost_estimate=cost(2 * GROUP * TOK * ROWS * EXPERTS * 128, 4 * 1024 * 1024),
    )(ids, weights, x, route)


def second_sums(ids, weights, x, place, parts):
    vmem = pl.BlockSpec(memory_space=pltpu.VMEM)
    return pl.pallas_call(
        second_kernel,
        out_shape=jax.ShapeDtypeStruct((GROUP * TOK, 128), bf16),
        in_specs=[pl.BlockSpec(memory_space=pltpu.SMEM)] + [vmem] * 4,
        out_specs=vmem,
        scratch_shapes=[pltpu.VMEM((GROUP * TOK, 128), bf16)] * 2,
        compiler_params=params(20),
        cost_estimate=cost(2 * GROUP * TOK * ROWS * EXPERTS * 128, 4 * 1024 * 1024),
    )(ids, weights, x, place, parts)


def hidden_kernel(p_ref, route_ref, prob_ref, h_ref, wide_ref):
    total = p_ref[0].astype(f32)
    for i in range(1, GROUP):
        total = total + p_ref[i].astype(f32)
    gate = total[:, :UNITS]
    up = total[:, UNITS:]
    hidden = gate * jax.nn.sigmoid(gate) * up
    rows = [jnp.broadcast_to(r, (4, TOK)) for r in (route_ref[...].astype(f32), prob_ref[...])]
    columns = jnp.transpose(jnp.concatenate(rows, axis=0))
    route = jnp.broadcast_to(columns[:, 0:1], (TOK, UNITS))
    wide_ref[...] = jnp.broadcast_to(columns[:, 4:5], (TOK, 128))
    for j in range(XH):
        for y in range(Y):
            at = (j * Y + y) * UNITS
            h_ref[:, at : at + UNITS] = jnp.where(route == 2.0 * y + j, hidden, 0.0).astype(bf16)


def hidden_units(parts, route_row, prob_row):
    return pl.pallas_call(
        hidden_kernel,
        out_shape=(
            jax.ShapeDtypeStruct((TOK, EXPERTS * UNITS), bf16),
            jax.ShapeDtypeStruct((TOK, 128), f32),
        ),
        compiler_params=params(6),
        cost_estimate=cost(0, GROUP * TOK * 256),
    )(parts, route_row, prob_row)


def finish_kernel(h_ref, prob_ref, d_ref, o_ref, w_scr, sems):
    step = pl.program_id(0)
    n = Z // pl.num_programs(0)

    def weights(z):
        return pltpu.make_async_copy(d_ref.at[z], w_scr.at[z], sems.at[z])

    @pl.when(step == 0)
    def _():
        for z in range(Z):
            weights(z).start()

    prob = jnp.concatenate([prob_ref[...]] * 5, axis=1)
    split = Y * UNITS
    lane = lax.broadcasted_iota(jnp.int32, (split, 128), 1)

    def beside(left, right):
        middle = jnp.where(lane < UNITS, left[:, 256:384].astype(f32), right[:, 256:384].astype(f32))
        return jnp.concatenate([left[:, :256], middle.astype(bf16), right[:, 384:]], axis=1)

    for k in range(n):
        z = step * n + k
        weights(z).wait()
        even = w_scr[z, :, 0].reshape(split, 2 * COLS)
        odd = w_scr[z, :, 1].reshape(split, 2 * COLS)
        low = jnp.dot(h_ref[:, :split], beside(even, odd), preferred_element_type=f32)
        high = jnp.dot(h_ref[:, split:], beside(odd, even), preferred_element_type=f32)
        total = low + jnp.concatenate([high[:, COLS:], high[:, :COLS]], axis=1)
        total = total.astype(bf16)
        blocks = [total[:, i * ROWS : (i + 1) * ROWS] for i in (0, 2, 1, 3)]
        whole = jnp.concatenate(blocks, axis=1).astype(f32)
        o_ref[:, k * 2 * COLS : (k + 1) * 2 * COLS] = (prob * whole).astype(bf16)


def finish(hidden, prob, down):
    steps = 4
    return pl.pallas_call(
        finish_kernel,
        out_shape=jax.ShapeDtypeStruct((TOK, D), bf16),
        grid=(steps,),
        in_specs=[
            pl.BlockSpec((TOK, EXPERTS * UNITS), lambda i: (0, 0)),
            pl.BlockSpec((TOK, 128), lambda i: (0, 0)),
            pl.BlockSpec(memory_space=pl.ANY),
        ],
        out_specs=pl.BlockSpec((TOK, D // steps), lambda i: (0, i)),
        scratch_shapes=[
            pltpu.VMEM((Z, Y, C, UNITS, 2 * COLS), bf16),
            pltpu.SemaphoreType.DMA((Z,)),
        ],
        compiler_params=params(52),
        cost_estimate=cost(2 * TOK * EXPERTS * UNITS * D, 12 * 1024 * 1024),
    )(hidden, prob, down)


def shards(grad_parts, master, moment, second, down_weight, tokens, routes, probs):
    core = lax.axis_index("c")
    low = lax.axis_index("xl")
    high = lax.axis_index("xh")
    core_id = core.reshape(1).astype(jnp.int32)
    group = ("z", "xl")

    grads = grad_parts.reshape(GROUP, C, ROWS, 128)
    sent = lax.dynamic_index_in_dim(grads, 1 - core, axis=1, keepdims=False)
    received = lax.ppermute(sent, "c", SWAP)

    down = jnp.broadcast_to(down_weight[0].T[None], (XH * XL, UNITS, ROWS))
    four = lax.all_to_all(down, ("xh", "xl"), 0, 0, tiled=True)
    pair = jnp.transpose(four, (1, 0, 2)).reshape(UNITS, 2 * COLS)
    pair = jnp.where(core == 0, pair, jnp.concatenate([pair[:, COLS:], pair[:, :COLS]], 1))
    pair, received = lax.optimization_barrier((pair, received))
    down_all = lax.all_gather(pair, ("z", "y", "c"), axis=0, tiled=False)
    down_all = down_all.reshape(Z, Y, C, UNITS, 2 * COLS)
    chunk = add(core_id, grads, received, routes.reshape(1, TOK))
    arrived = lax.all_to_all(chunk, group, 0, 0, tiled=True)
    packed, arrived = lax.optimization_barrier((pack(tokens), arrived))
    columns = lax.all_to_all(packed, group, 0, 0, tiled=True)

    new_master, new_moment, short, route_all = adam(arrived, master[0], moment[0], second[0])
    pair_short = jnp.concatenate([short, lax.ppermute(short, "xh", SWAP)], axis=0)
    own = lax.all_gather(pair_short, "y", axis=0, tiled=True).reshape(EXPERTS, ROWS, 128)
    other = lax.ppermute(own, "c", SWAP)

    ids = jnp.stack([core, high]).astype(jnp.int32)
    parts, place = first_sums(ids, own, columns, route_all)
    parts = second_sums(ids, other, columns, place, parts)
    parts = lax.all_to_all(parts.reshape(GROUP, TOK, 128), group, 0, 0, tiled=True)
    hidden, prob = hidden_units(parts, routes.reshape(1, TOK), probs.reshape(1, TOK))
    mixed = finish(hidden, prob, down_all)
    return new_master[None], new_moment[None], mixed


def solution(mesh):
    fine = Mesh(mesh.devices.reshape(Z, XL, C, Y, XH), ("z", "xl", "c", "y", "xh"))
    dp, expert = ("z", "xl", "c"), ("y", "xh")
    both = dp + expert
    in_specs = (
        P(expert, dp, None, None),
        P(expert, dp, None),
        P(expert, dp, None),
        P(expert, dp, None),
        P(expert, dp, None),
        P(both, None),
        P(both, None),
        P(both),
    )
    out_specs = (P(expert, dp, None), P(expert, dp, None), P(both, None))
    return jax.shard_map(shards, mesh=fine, in_specs=in_specs, out_specs=out_specs, check_vma=False)
```
